256 devices in a mesh: rows: 64 (over y_lo, z, x), cols: 4 (over y_hi, core).
Axes of the slice: x: 4, y: 4 (y_hi: 2, y_lo: 2; y = y_hi * 2 + y_lo), z: 8, core: 2. Of those that a mesh axis runs over, the one named last changes fastest.
Arguments:
- inputs: bfloat16 [2, 256, 512, 512], P(None, 'rows', 'cols'), may hold values from -6 to 6
- tight_conv_kernel: bfloat16 [3, 3, 512, 512], P(None, None, 'rows'), may hold values from -0.09375 to 0.09375
- wide_conv_kernel: bfloat16 [3, 3, 512, 512], P(None, None, 'rows'), may hold values from -0.09375 to 0.09375
- up_weight: bfloat16 [512, 2048], P(None, 'rows'), may hold values from -0.25 to 0.25
- down_weight: bfloat16 [2048, 512], P('rows'), may hold values from -0.125 to 0.125
Outputs:
- outputs: bfloat16 [2, 256, 512, 512], P(None, 'rows', 'cols')
The draws below stay inside these ranges and needn't reach their ends.
All inputs are finite; a program needn't handle non-finite values.
Results may differ from the reference program's by a relative error of at most 0.007.
Values may be sent and summed in bfloat16 or wider, within the bound.
No kernel may reach another device: no remote copies, remote signals or barrier semaphores. Data moves between devices by JAX's collectives and lax.ppermute only.
A program may use at most 64 MiB of HBM per device.

```python
import jax
import jax.numpy as jnp
from jax import lax

C = 512
FF = 2048
H = 256
W = 512
TIGHT_DILATION = 16
WIDE_DILATION = 64
SAMPLES = 2


def level_of(stream_key, shape, shards, smallest, largest):
    gain, own = 1.0, jax.random.fold_in(stream_key, 6)
    for dim, shards_of in shards:
        draws = jnp.exp(jax.random.uniform(jax.random.fold_in(own, dim), (shards_of,), jnp.float32, smallest / len(shards), largest / len(shards)))
        gain = gain * jnp.repeat(draws, shape[dim] // shards_of).reshape([-1 if axis == dim else 1 for axis in range(len(shape))])
    return gain


def scatter_about(stream_key, dims, width, limit, shards=(), kind=jnp.bfloat16):
    entries = jax.random.normal(stream_key, dims, jnp.float32) * width
    if len(shards) > 0:
        entries = level_of(stream_key, dims, shards, -0.22, 0.18) * entries
    return jnp.clip(entries, min=-limit, max=limit).astype(kind)


def setup_inputs(seed: int = 0) -> dict:
    seeds = jax.random.split(jax.random.key(seed), 6)
    inputs = scatter_about(seeds[0], (SAMPLES, H, W, C), 1.0, 6.0, ((1, 64), (2, 4)))
    tight_conv_kernel = scatter_about(seeds[1], (3, 3, C, C), (9 * C) ** -0.5, 0.09375, ((2, 64),))
    wide_conv_kernel = scatter_about(seeds[2], (3, 3, C, C), (9 * C) ** -0.5, 0.09375, ((2, 64),))
    up_weight = scatter_about(seeds[3], (C, FF), C ** -0.5, 0.25, ((1, 64),))
    down_weight = scatter_about(seeds[4], (FF, C), FF ** -0.5, 0.125, ((0, 64),))
    return {"inputs": inputs, "tight_conv_kernel": tight_conv_kernel, "wide_conv_kernel": wide_conv_kernel, "up_weight": up_weight, "down_weight": down_weight}


def rms_scaled_rows(values):
    widened = values.astype(jnp.float32)
    scaled = widened * lax.rsqrt(lax.optimization_barrier(jnp.mean(widened * widened, axis=-1, keepdims=True)) + 1e-06)
    return scaled.astype(jnp.bfloat16)

def dilated_conv_output(normed, weight, spread):
    height, col_count, channel_count = normed.shape
    padded = jnp.pad(normed, ((spread, spread), (spread, spread), (0, 0)))
    summed = jnp.zeros((height * col_count, channel_count), jnp.float32)
    for row_index in range(3):
        for col_index in range(3):
            window = padded[row_index * spread:row_index * spread + height, col_index * spread:col_index * spread + col_count]
            window = window.reshape(height * col_count, channel_count)
            summed = summed + jnp.dot(window, weight[row_index, col_index], preferred_element_type=jnp.float32)
    return summed.reshape(height, col_count, channel_count)

def one_sample(single_example, tight_conv_kernel, wide_conv_kernel, up_weight, down_weight):
    tight_conv_result = (single_example.astype(jnp.float32) + dilated_conv_output(rms_scaled_rows(single_example), tight_conv_kernel, TIGHT_DILATION)).astype(jnp.bfloat16)
    wide_conv_result = (tight_conv_result.astype(jnp.float32) + dilated_conv_output(rms_scaled_rows(tight_conv_result), wide_conv_kernel, WIDE_DILATION)).astype(jnp.bfloat16)
    mlp_input = rms_scaled_rows(wide_conv_result).reshape(-1, wide_conv_result.shape[2])
    hidden = jax.nn.gelu(jnp.dot(mlp_input, up_weight, preferred_element_type=jnp.float32)).astype(jnp.bfloat16)
    branch = jnp.dot(hidden, down_weight, preferred_element_type=jnp.float32).reshape(wide_conv_result.shape)
    return (wide_conv_result.astype(jnp.float32) + branch).astype(jnp.bfloat16)

def reference(inputs, tight_conv_kernel, wide_conv_kernel, up_weight, down_weight):
    return lax.map(lambda single_example: one_sample(single_example, tight_conv_kernel, wide_conv_kernel, up_weight, down_weight), inputs)
```

```python
import jax
import jax.numpy as jnp
import numpy as np
from jax import lax
from jax.sharding import Mesh, PartitionSpec as P

AXES = ("ylo", "z", "x", "yhi", "core")
SIZES = (2, 8, 4, 2, 2)
PEERS = ("ylo", "z", "yhi", "core")


def neighbour_groups():
    groups = {"y": [], "xy": []}
    for z in range(8):
        for core in range(2):
            for first in (0, 2):
                ys = [(first + core) % 4, (first + core + 1) % 4]
                ys.sort(key=lambda y: y % 2)
                at = lambda y, x: int(np.ravel_multi_index((y % 2, z, x, y // 2, core), SIZES))
                for x in range(4):
                    groups["y"].append([at(y, x) for y in ys])
                groups["xy"].append([at(y, x) for y in ys for x in range(4)])
    return groups


GROUPS = neighbour_groups()


def spread(piece, axis, count, groups=None):
    copies = jnp.broadcast_to(piece[None], (count,) + piece.shape)
    return lax.all_to_all(copies, axis, 0, 0, axis_index_groups=groups)


def rms_normalize(values):
    widened = values.astype(jnp.float32)
    scaled = widened * lax.rsqrt(jnp.mean(widened * widened, axis=-1, keepdims=True) + 1e-06)
    return scaled.astype(jnp.bfloat16)


def conv(cells, kernel, step):
    r, c, b, ch = cells.shape
    padded = jnp.pad(cells, ((step, step), (step, step), (0, 0), (0, 0)))
    total = jnp.zeros((r * c * b, kernel.shape[-1]), jnp.float32)
    for i in range(3):
        for j in range(3):
            window = padded[i * step : i * step + r, j * step : j * step + c].reshape(-1, ch)
            total = total + jnp.dot(window, kernel[i, j], preferred_element_type=jnp.float32)
    return total.reshape(r, c, b, -1)


def shards(inputs, tight, wide, up, down):
    core = lax.axis_index("core")
    s, i, cols, ch = inputs.shape
    def half_out(k):
        return lax.dynamic_slice_in_dim(k, core * (ch // 2), ch // 2, axis=3)
    t_half, w_half = half_out(tight), half_out(wide)
    n = down.shape[0] // 2
    f_half = jnp.stack([lax.dynamic_slice_in_dim(up.T, core * n, n, 0), lax.dynamic_slice_in_dim(down, core * n, n, 0)])

    t_z = spread(t_half, "z", 8)
    cells = inputs.reshape(s, i, 8, 8, 2, ch).transpose(0, 1, 3, 2, 4, 5).reshape(64, 16, ch)
    cells = lax.all_to_all(cells, PEERS, 0, 0).reshape(16, 32, 2, ch)
    t_yx = spread(t_z, AXES, 8, GROUPS["xy"])
    t_all = spread(t_yx, "core", 2).reshape(2, 2, 4, 8, 3, 3, 8, ch // 2)
    tight_full = t_all.transpose(4, 5, 1, 3, 2, 6, 0, 7).reshape(3, 3, ch, ch)

    w_z = spread(w_half, "z", 8)
    w_x = spread(w_z, "x", 4)
    w_y = spread(w_x, AXES, 2, GROUPS["y"])
    w_all = spread(w_y, "core", 2)
    wide_full = w_all.transpose(4, 5, 1, 3, 2, 6, 0, 7).reshape(3, 3, ch, ch)

    f_z = spread(f_half, "z", 8)
    f_x = spread(f_z, "x", 4)
    f_y = spread(f_x, AXES, 2, GROUPS["y"])
    f_all = spread(f_y, "core", 2)
    f_all = f_all.transpose(4, 0, 1, 2, 3, 5, 6).reshape(2, -1, ch)

    near = (cells.astype(jnp.float32) + conv(rms_normalize(cells), tight_full, 1)).astype(jnp.bfloat16)
    far = (near.astype(jnp.float32) + conv(rms_normalize(near), wide_full, 4)).astype(jnp.bfloat16)
    rows = rms_normalize(far).reshape(-1, ch)
    hidden = lax.dot_general(rows, f_all[0], (((1,), (1,)), ((), ())), preferred_element_type=jnp.float32)
    hidden = jax.nn.gelu(hidden).astype(jnp.bfloat16)
    branch = jnp.dot(hidden, f_all[1], preferred_element_type=jnp.float32)
    out = (far.astype(jnp.float32) + branch.reshape(far.shape)).astype(jnp.bfloat16)
    out = lax.all_to_all(out.reshape(64, 16, ch), PEERS, 0, 0)
    return out.reshape(s, i, 8, 8, 2, ch).transpose(0, 1, 3, 2, 4, 5).reshape(inputs.shape)


def solution(mesh):
    grid = Mesh(mesh.devices.reshape(SIZES), AXES)
    rows, columns = ("ylo", "z", "x"), ("yhi", "core")
    placed = (
        P(None, rows, columns, None),
        P(None, None, rows, None),
        P(None, None, rows, None),
        P(None, rows),
        P(rows, None),
    )
    return jax.shard_map(shards, mesh=grid, in_specs=placed, out_specs=P(None, rows, columns, None), check_vma=False)
```

```python
import functools

import jax
import jax.numpy as jnp
import numpy as np
from jax import lax
from jax.experimental import pallas as pl
from jax.experimental.pallas import tpu as pltpu
from jax.sharding import Mesh, PartitionSpec as P

AXES = ("ylo", "z", "x", "yhi", "core")
SIZES = (2, 8, 4, 2, 2)
PEERS = ("ylo", "z", "yhi", "core")
ROWS, COLS, PAIR = 16, 32, 2
LINE = COLS * PAIR
TAPS = 9
VMEM_LIMIT = 56 * 1024 * 1024


def moved(array, to):
    pairs = []
    for source, (ylo, z, x, yhi, core) in enumerate(np.ndindex(SIZES)):
        y, z, x, core = to(2 * yhi + ylo, z, x, core)
        y, z, x, core = y % 4, z % 8, x % 4, core % 2
        pairs.append((source, int(np.ravel_multi_index((y % 2, z, x, y // 2, core), SIZES))))
    return lax.ppermute(array, AXES, pairs)


def over_x(piece):
    parts = [piece] + [moved(piece, lambda y, z, x, c, k=k: (y, z, x + k, c)) for k in (1, 2, 3)]
    return jnp.stack(parts)


def over_z(piece):
    parts = [piece] + [moved(piece, lambda y, z, x, c, k=k: (y, z + k, x, c)) for k in range(1, 8)]
    return jnp.stack(parts)


def from_y(piece):
    return moved(piece, lambda y, z, x, c: (y + 1 - 2 * c, z, x, c))


def from_core(piece):
    return moved(piece, lambda y, z, x, c: (y, z, x, 1 - c))


def normalized(values):
    return values * lax.rsqrt(jnp.mean(values * values, axis=-1, keepdims=True) + 1e-06)


def conv_kernel(step, where, cells, *refs):
    weights, (out, shifted, kernel, total, sems) = refs[:4], refs[4:]
    x, ylo, core = where[0], where[1], where[2]
    copies = []
    for n, source in enumerate(weights):
        c = core if n < 2 else 1 - core
        y = ylo if n % 2 == 0 else 1 - ylo
        for k in range(4):
            copies.append(
                pltpu.make_async_copy(
                    source.at[k], kernel.at[c, :, y, :, (x + 4 - k) % 4], sems.at[n * 4 + k]
                )
            )
    for copy in copies:
        copy.start()
    ch = cells.shape[-1]
    blank = jnp.zeros((step, LINE, ch), jnp.bfloat16)
    for j in range(3):
        shifted[j, pl.ds(0, step)] = blank
        shifted[j, pl.ds(ROWS + step, step)] = blank
    column = lax.broadcasted_iota(jnp.int32, (LINE, ch), 0)
    by = step * PAIR

    def fill(r, _):
        row = normalized(cells[r].astype(jnp.float32))
        before = jnp.where(column >= by, pltpu.roll(row, by, 0), 0.0)
        after = jnp.where(column < LINE - by, pltpu.roll(row, LINE - by, 0), 0.0)
        shifted[0, r + step] = before.astype(jnp.bfloat16)
        shifted[1, r + step] = row.astype(jnp.bfloat16)
        shifted[2, r + step] = after.astype(jnp.bfloat16)
        return 0

    lax.fori_loop(0, ROWS, fill, 0)
    for copy in copies:
        copy.wait()
    half = ch // 2
    for c in range(2):
        total[c] = cells[...].reshape(ROWS * LINE, ch)[:, c * half : (c + 1) * half].astype(jnp.float32)

    def tap(t, _):
        i, j = t // 3, t % 3
        window = shifted[j, pl.ds(i * step, ROWS)].reshape(ROWS * LINE, ch)
        for c in range(2):
            part = kernel[c, t].reshape(ch, half)
            total[c] += jnp.dot(window, part, preferred_element_type=jnp.float32)
        return 0

    lax.fori_loop(0, TAPS, tap, 0)
    for c in range(2):
        out[:, :, c * half : (c + 1) * half] = total[c].astype(jnp.bfloat16).reshape(ROWS, LINE, half)


def conv_block(cells, weights, step, where):
    ch = cells.shape[-1]
    whole = pl.BlockSpec(memory_space=pltpu.VMEM)
    return pl.pallas_call(
        functools.partial(conv_kernel, step),
        out_shape=jax.ShapeDtypeStruct(cells.shape, jnp.bfloat16),
        in_specs=[pl.BlockSpec(memory_space=pltpu.SMEM), whole] + [pl.BlockSpec(memory_space=pl.ANY)] * 4,
        out_specs=whole,
        scratch_shapes=[
            pltpu.VMEM((3, ROWS + 2 * step, LINE, ch), jnp.bfloat16),
            pltpu.VMEM((2, TAPS, 2, 8, 4, 8, ch // 2), jnp.bfloat16),
            pltpu.VMEM((2, ROWS * LINE, ch // 2), jnp.float32),
            pltpu.SemaphoreType.DMA((16,)),
        ],
        compiler_params=pltpu.CompilerParams(vmem_limit_bytes=VMEM_LIMIT),
        cost_estimate=pl.CostEstimate(
            flops=2 * TAPS * ROWS * LINE * ch * ch, bytes_accessed=7 * 2**20, transcendentals=0
        ),
    )(where, cells, *weights)


def ffn_kernel(cells, *refs):
    pieces, (out, held, total, sems) = refs[:4], refs[4:]
    copies = [pltpu.make_async_copy(piece, held.at[n], sems.at[n]) for n, piece in enumerate(pieces)]
    for copy in copies:
        copy.start()
    ch = cells.shape[-1]
    total[...] = cells[...].reshape(-1, ch).astype(jnp.float32)
    rows = normalized(total[...]).astype(jnp.bfloat16)
    for n in range(4):
        copies[n].wait()
        up = held[n, :, 0].reshape(-1, ch)
        down = held[n, :, 1].reshape(-1, ch)
        hidden = lax.dot_general(rows, up, (((1,), (1,)), ((), ())), preferred_element_type=jnp.float32)
        hidden = jax.nn.gelu(hidden).astype(jnp.bfloat16)
        total[...] += jnp.dot(hidden, down, preferred_element_type=jnp.float32)
    out[...] = total[...].astype(jnp.bfloat16).reshape(out.shape)


def ffn_block(cells, pieces):
    ch = cells.shape[-1]
    whole = pl.BlockSpec(memory_space=pltpu.VMEM)
    return pl.pallas_call(
        ffn_kernel,
        out_shape=jax.ShapeDtypeStruct(cells.shape, jnp.bfloat16),
        in_specs=[whole] + [pl.BlockSpec(memory_space=pl.ANY)] * 4,
        out_specs=whole,
        scratch_shapes=[
            pltpu.VMEM((4,) + pieces[0].shape, jnp.bfloat16),
            pltpu.VMEM((ROWS * LINE, ch), jnp.float32),
            pltpu.SemaphoreType.DMA((4,)),
        ],
        compiler_params=pltpu.CompilerParams(vmem_limit_bytes=VMEM_LIMIT),
        cost_estimate=pl.CostEstimate(
            flops=4 * ROWS * LINE * ch * 4 * ch, bytes_accessed=6 * 2**20, transcendentals=ROWS * LINE * 4 * ch
        ),
    )(cells, *pieces)


def shards(inputs, tight, wide, up, down):
    core = lax.axis_index("core")
    where = jnp.stack([lax.axis_index("x"), lax.axis_index("ylo"), core]).astype(jnp.int32)
    s, i, cols, ch = inputs.shape
    n = down.shape[0] // 2
    both = jnp.stack([tight, wide]).reshape(2, TAPS, -1, ch)
    both = lax.dynamic_slice_in_dim(both, core * (ch // 2), ch // 2, axis=3)
    mlp = jnp.stack([lax.dynamic_slice_in_dim(up.T, core * n, n, 0), lax.dynamic_slice_in_dim(down, core * n, n, 0)])

    cells = inputs.reshape(s, i, 8, 8, PAIR, ch).transpose(0, 1, 3, 2, 4, 5).reshape(64, 16, ch)
    both_z = lax.all_to_all(jnp.broadcast_to(both[None], (8,) + both.shape), "z", 0, 0)
    both_z, cells, mlp = lax.optimization_barrier((both_z, cells, mlp))
    both_z = both_z.transpose(1, 2, 0, 3, 4)
    cells = lax.all_to_all(cells, PEERS, 0, 0).reshape(ROWS, LINE, ch)

    t_own = over_x(both_z[0])
    t_other = over_x(from_y(both_z[0]))
    tight_parts = [t_own, t_other, from_core(t_own), from_core(t_other)]

    w_own = over_x(both_z[1])
    w_other = from_y(w_own)
    wide_parts = [w_own, w_other, from_core(w_own), from_core(w_other)]

    f_z = over_z(mlp).transpose(1, 0, 2, 3)
    f_own = over_x(f_z)
    f_other = from_y(f_own)
    mlp_parts = [f_own, f_other, from_core(f_own), from_core(f_other)]

    near = conv_block(cells, tight_parts, 1, where)
    far = conv_block(near, wide_parts, 4, where)
    out = ffn_block(far, mlp_parts)
    out = lax.all_to_all(out.reshape(64, 16, ch), PEERS, 0, 0)
    return out.reshape(s, i, 8, 8, PAIR, ch).transpose(0, 1, 3, 2, 4, 5).reshape(inputs.shape)


def solution(mesh):
    grid = Mesh(mesh.devices.reshape(SIZES), AXES)
    rows, columns = ("ylo", "z", "x"), ("yhi", "core")
    placed = (
        P(None, rows, columns, None),
        P(None, None, rows, None),
        P(None, None, rows, None),
        P(None, rows),
        P(rows, None),
    )
    return jax.shard_map(shards, mesh=grid, in_specs=placed, out_specs=P(None, rows, columns, None), check_vma=False)
```

```python
import functools

import jax
import jax.numpy as jnp
import numpy as np
from jax import lax
from jax.experimental import pallas as pl
from jax.experimental.pallas import tpu as pltpu
from jax.sharding import Mesh, PartitionSpec as P

AXES = ("ylo", "z", "x", "yhi", "core")
SIZES = (2, 8, 4, 2, 2)
PEERS = ("ylo", "z", "yhi", "core")
ROWS, COLS, PAIR = 16, 32, 2
LINE = COLS * PAIR
CELLS = ROWS * LINE
TAPS = 9
MLP = 8
VMEM_LIMIT = 56 * 1024 * 1024


def moved(array, to):
    pairs = []
    for source, (ylo, z, x, yhi, core) in enumerate(np.ndindex(SIZES)):
        y, z, x, core = to(2 * yhi + ylo, z, x, core)
        y, z, x, core = y % 4, z % 8, x % 4, core % 2
        pairs.append((source, int(np.ravel_multi_index((y % 2, z, x, y // 2, core), SIZES))))
    return lax.ppermute(array, AXES, pairs)


def from_x(piece, turn):
    return moved(piece, lambda y, z, x, c: (y, z, x ^ (3 if c != turn else 1), c))


def from_z(piece, bit):
    def partner(y, z, x, c):
        if bit == 2:
            return y, z ^ 4, x, c
        if bit == 1:
            return y, z ^ (6 if c else 2), x, c
        return y, z + (1 if (z + c) % 2 == 0 else -1), x, c

    return moved(piece, partner)


def joined(mine, theirs, place):
    pair = [jnp.where(place == 0, mine, theirs), jnp.where(place == 0, theirs, mine)]
    n, pieces, rows, width = mine.shape
    return jnp.stack(pair, axis=2).reshape(n, 2 * pieces, rows, width)


def from_y(piece):
    return moved(piece, lambda y, z, x, c: (y + 1 - 2 * c, z, x, c))


def from_core(piece):
    return moved(piece, lambda y, z, x, c: (y, z, x, 1 - c))


def x_slots(x, core):
    first = jnp.where(core == 0, x ^ 1, x ^ 3)
    return x, first, x ^ first ^ (x ^ 2), x ^ 2


def normalized(values):
    return values * lax.rsqrt(jnp.mean(values * values, axis=-1, keepdims=True) + 1e-06)


def weight_copies(split_y, where, sources, kernel, sems):
    x, ylo, core = where[0], where[1], where[2]
    copies = []

    def add(source, c, y, at):
        copies.append(pltpu.make_async_copy(source, kernel.at[c, :, y, :, at], sems.at[len(copies)]))

    for far in range(2):
        c = core if far == 0 else 1 - core
        slots = x_slots(x, c)
        for y in range(2):
            y_of = ylo if y == 0 else 1 - ylo
            for part in range(2):
                for k in range(2):
                    if split_y:
                        source = sources[far * 4 + y * 2 + part].at[k, pl.ds(0, TAPS)]
                    else:
                        source = sources[far * 2 + part].at[k, y]
                    add(source, c, y_of, slots[part * 2 + k])
    return copies


def conv_kernel(step, split_y, n_weights, where, cells, *refs):
    weights, (out, shifted, kernel, total, sems) = refs[:n_weights], refs[n_weights:]
    copies = weight_copies(split_y, where, weights, kernel, sems)
    for copy in copies:
        copy.start()
    ch = cells.shape[-1]
    half = ch // 2
    blank = jnp.zeros((step, LINE, 3 * ch), jnp.bfloat16)
    shifted[pl.ds(0, step)] = blank
    shifted[pl.ds(ROWS + step, step)] = blank
    column = lax.broadcasted_iota(jnp.int32, (LINE, ch), 0)
    by = step * PAIR

    def fill(r, _):
        raw = cells[r].astype(jnp.float32)
        for c in range(2):
            total[c, pl.ds(r * LINE, LINE)] = raw[:, c * half : (c + 1) * half]
        row = normalized(raw)
        before = jnp.where(column >= by, pltpu.roll(row, by, 0), 0.0)
        after = jnp.where(column < LINE - by, pltpu.roll(row, LINE - by, 0), 0.0)
        for j, values in enumerate((before, row, after)):
            shifted[r + step, :, j * ch : (j + 1) * ch] = values.astype(jnp.bfloat16)
        return 0

    lax.fori_loop(0, ROWS, fill, 0)
    for copy in copies:
        copy.wait()

    def taps(i, _):
        window = shifted[pl.ds(i * step, ROWS)].reshape(CELLS, 3 * ch)
        for c in range(2):
            part = kernel[c, pl.ds(3 * i, 3)].reshape(3 * ch, half)
            total[c] += jnp.dot(window, part, preferred_element_type=jnp.float32)
        return 0

    lax.fori_loop(0, 3, taps, 0)
    for c in range(2):
        out[:, :, c * half : (c + 1) * half] = total[c].astype(jnp.bfloat16).reshape(ROWS, LINE, half)


def conv_block(cells, weights, step, split_y, where):
    ch = cells.shape[-1]
    whole = pl.BlockSpec(memory_space=pltpu.VMEM)
    return pl.pallas_call(
        functools.partial(conv_kernel, step, split_y, len(weights)),
        out_shape=jax.ShapeDtypeStruct(cells.shape, jnp.bfloat16),
        in_specs=[pl.BlockSpec(memory_space=pltpu.SMEM), whole] + [pl.BlockSpec(memory_space=pl.ANY)] * len(weights),
        out_specs=whole,
        scratch_shapes=[
            pltpu.VMEM((ROWS + 2 * step, LINE, 3 * ch), jnp.bfloat16),
            pltpu.VMEM((2, TAPS, 2, 8, 4, 8, ch // 2), jnp.bfloat16),
            pltpu.VMEM((2, CELLS, ch // 2), jnp.float32),
            pltpu.SemaphoreType.DMA((16,)),
        ],
        compiler_params=pltpu.CompilerParams(vmem_limit_bytes=VMEM_LIMIT),
        cost_estimate=pl.CostEstimate(
            flops=1000, bytes_accessed=1000, transcendentals=0
        ),
    )(where, cells, *weights)


def ffn_kernel(cells, *refs):
    pieces, (out, held, total, sems) = refs[:8], refs[8:]
    copies = []
    for n, piece in enumerate(pieces):
        group = []
        for part in range(4):
            group.append(
                pltpu.make_async_copy(
                    piece.at[:, pl.ds(TAPS + 2 * part, 2)], held.at[part // 2, part % 2, n], sems.at[n * 4 + part]
                )
            )
        copies.append(group)
    for group in copies:
        for copy in group:
            copy.start()
    ch = cells.shape[-1]
    half = ch // 2
    raw = cells[...].reshape(CELLS, ch).astype(jnp.float32)
    rows = normalized(raw).astype(jnp.bfloat16)
    for c in range(2):
        total[c] = raw[:, c * half : (c + 1) * half]
    for n in range(0, 8, 2):
        for copy in copies[n] + copies[n + 1]:
            copy.wait()
        hidden = None
        for c in range(2):
            up = held[c, 0, n : n + 2].reshape(-1, half)
            part = lax.dot_general(
                rows[:, c * half : (c + 1) * half], up, (((1,), (1,)), ((), ())), preferred_element_type=jnp.float32
            )
            hidden = part if hidden is None else hidden + part
        hidden = jax.nn.gelu(hidden).astype(jnp.bfloat16)
        for c in range(2):
            down = held[c, 1, n : n + 2].reshape(-1, half)
            total[c] += jnp.dot(hidden, down, preferred_element_type=jnp.float32)
    for c in range(2):
        out[:, :, c * half : (c + 1) * half] = total[c].astype(jnp.bfloat16).reshape(ROWS, LINE, half)


def ffn_block(cells, pieces):
    ch = cells.shape[-1]
    whole = pl.BlockSpec(memory_space=pltpu.VMEM)
    return pl.pallas_call(
        ffn_kernel,
        out_shape=jax.ShapeDtypeStruct(cells.shape, jnp.bfloat16),
        in_specs=[whole] + [pl.BlockSpec(memory_space=pl.ANY)] * 8,
        out_specs=whole,
        scratch_shapes=[
            pltpu.VMEM((2, 2, 8, 2, 2, 8, 8, ch // 2), jnp.bfloat16),
            pltpu.VMEM((2, CELLS, ch // 2), jnp.float32),
            pltpu.SemaphoreType.DMA((32,)),
        ],
        compiler_params=pltpu.CompilerParams(vmem_limit_bytes=VMEM_LIMIT),
        cost_estimate=pl.CostEstimate(
            flops=1000, bytes_accessed=1000, transcendentals=0
        ),
    )(cells, *pieces)


def shards(inputs, tight, wide, up, down):
    core = lax.axis_index("core")
    where = jnp.stack([lax.axis_index("x"), lax.axis_index("ylo"), core]).astype(jnp.int32)
    s, i, cols, ch = inputs.shape
    half, n = ch // 2, down.shape[0] // 2
    kernels = jnp.concatenate([tight.reshape(TAPS, 8, ch), wide.reshape(TAPS, 8, ch)])
    kernels = lax.dynamic_slice_in_dim(kernels, core * half, half, axis=2)
    mlp = jnp.stack([lax.dynamic_slice_in_dim(up.T, core * n, n, 0), lax.dynamic_slice_in_dim(down, core * n, n, 0)])
    mlp = jnp.stack([mlp[:, :, :half], mlp[:, :, half:]]).reshape(MLP, 8, half)
    shard = jnp.concatenate([kernels, mlp])

    cells = inputs.reshape(s, i, 8, 8, PAIR, ch).transpose(0, 1, 3, 2, 4, 5).reshape(64, 16, ch)
    shard = shard.reshape(-1, 1, 8, half)
    for bit in (2, 1, 0):
        shard = joined(shard, from_z(shard, bit), (lax.axis_index("z") >> bit) & 1)
    shard = shard.reshape(-1, 8, 8, half)
    shard, cells = lax.optimization_barrier((shard, cells))
    cells = lax.all_to_all(cells, PEERS, 0, 0).reshape(ROWS, LINE, ch)

    near_half = jnp.stack([shard[:TAPS], from_y(shard[:TAPS])])
    rest = shard[TAPS:]
    first = jnp.stack([rest, from_x(rest, 0)])
    second = from_x(first, 1)
    first_y = from_y(first)
    t_first = jnp.stack([near_half, from_x(near_half, 0)])
    t_second = from_x(t_first, 1)
    t_second, cells = lax.optimization_barrier((t_second, cells))
    tight_parts = [t_first, t_second, from_core(t_first), from_core(t_second)]
    second, first_y = lax.optimization_barrier((second, first_y))
    own = [first, second, first_y, from_y(second)]
    parts = own + [from_core(piece) for piece in own]

    near = conv_block(cells, tight_parts, 1, False, where)
    far = conv_block(near, parts, 4, True, where)
    out = ffn_block(far, parts)
    out = lax.all_to_all(out.reshape(64, 16, ch), PEERS, 0, 0)
    return out.reshape(s, i, 8, 8, PAIR, ch).transpose(0, 1, 3, 2, 4, 5).reshape(inputs.shape)


def solution(mesh):
    grid = Mesh(mesh.devices.reshape(SIZES), AXES)
    rows, columns = ("ylo", "z", "x"), ("yhi", "core")
    placed = (
        P(None, rows, columns, None),
        P(None, None, rows, None),
        P(None, None, rows, None),
        P(None, rows),
        P(rows, None),
    )
    return jax.shard_map(shards, mesh=grid, in_specs=placed, out_specs=P(None, rows, columns, None), check_vma=False)
```

```python
import functools

import jax
import jax.numpy as jnp
import numpy as np
from jax import lax
from jax.experimental import pallas as pl
from jax.experimental.pallas import tpu as pltpu
from jax.sharding import Mesh, PartitionSpec as P

AXES = ("ylo", "z", "x", "yhi", "core")
SIZES = (2, 8, 4, 2, 2)
PEERS = ("ylo", "z", "yhi", "core")
ROWS, COLS, PAIR = 16, 32, 2
LINE = COLS * PAIR
CELLS = ROWS * LINE
TAPS = 9
MLP = 8
VMEM_LIMIT = 56 * 1024 * 1024


def moved(array, to):
    pairs = []
    for source, (ylo, z, x, yhi, core) in enumerate(np.ndindex(SIZES)):
        y, z, x, core = to(2 * yhi + ylo, z, x, core)
        y, z, x, core = y % 4, z % 8, x % 4, core % 2
        pairs.append((source, int(np.ravel_multi_index((y % 2, z, x, y // 2, core), SIZES))))
    return lax.ppermute(array, AXES, pairs)


def from_x(piece, turn):
    return moved(piece, lambda y, z, x, c: (y, z, x ^ (3 if c != turn else 1), c))


def from_z(piece, bit):
    def partner(y, z, x, c):
        if bit == 2:
            return y, z ^ 4, x, c
        if bit == 1:
            return y, z ^ (6 if c else 2), x, c
        return y, z + (1 if (z + c) % 2 == 0 else -1), x, c

    return moved(piece, partner)


def joined(mine, theirs, place):
    pair = [jnp.where(place == 0, mine, theirs), jnp.where(place == 0, theirs, mine)]
    n, pieces, rows, width = mine.shape
    return jnp.stack(pair, axis=2).reshape(n, 2 * pieces, rows, width)


def from_y(piece):
    return moved(piece, lambda y, z, x, c: (y + 1 - 2 * c, z, x, c))


def from_core(piece):
    return moved(piece, lambda y, z, x, c: (y, z, x, 1 - c))


def x_slots(x, core):
    first = jnp.where(core == 0, x ^ 1, x ^ 3)
    return x, first, x ^ first ^ (x ^ 2), x ^ 2


def normalized(values):
    return values * lax.rsqrt(jnp.mean(values * values, axis=-1, keepdims=True) + 1e-06)


def weight_copies(split_y, where, sources, kernel, sems):
    x, ylo, core = where[0], where[1], where[2]
    groups = [[], [], []]
    for i in range(3):
        taps = pl.ds(3 * i, 3)
        for far in range(2):
            c = core if far == 0 else 1 - core
            slots = x_slots(x, c)
            for y in range(2):
                y_of = ylo if y == 0 else 1 - ylo
                for part in range(2):
                    for k in range(2):
                        if split_y:
                            source = sources[far * 4 + y * 2 + part].at[k, taps]
                        else:
                            source = sources[far * 2 + part].at[k, y, taps]
                        place = kernel.at[c, taps, y_of, :, slots[part * 2 + k]]
                        groups[i].append(pltpu.make_async_copy(source, place, sems.at[i * 16 + len(groups[i])]))
    return groups


def convolve(step, cells, groups, shifted, kernel, total):
    ch = cells.shape[-1]
    half = ch // 2
    blank = jnp.zeros((step, LINE, 3 * ch), jnp.bfloat16)
    shifted[pl.ds(0, step)] = blank
    shifted[pl.ds(ROWS + step, step)] = blank
    by = step * PAIR

    def fill(r, _):
        raw = cells[r].astype(jnp.float32)
        for c in range(2):
            total[c, pl.ds(pl.multiple_of(r * LINE, LINE), LINE)] = raw[:, c * half : (c + 1) * half]
        row = normalized(raw)
        edge = jnp.zeros((by, ch), jnp.float32)
        if by % 8 == 0:
            before = jnp.concatenate([edge, row[: LINE - by]], axis=0)
            after = jnp.concatenate([row[by:], edge], axis=0)
        else:
            column = lax.broadcasted_iota(jnp.int32, (LINE, ch), 0)
            before = jnp.where(column >= by, pltpu.roll(row, by, 0), 0.0)
            after = jnp.where(column < LINE - by, pltpu.roll(row, LINE - by, 0), 0.0)
        for j, values in enumerate((before, row, after)):
            shifted[r + step, :, j * ch : (j + 1) * ch] = values.astype(jnp.bfloat16)
        return 0

    lax.fori_loop(0, ROWS, fill, 0)
    for i in range(3):
        for copy in groups[i]:
            copy.wait()
        window = shifted[pl.ds(i * step, ROWS)].reshape(CELLS, 3 * ch)
        for c in range(2):
            part = kernel[c, pl.ds(3 * i, 3)].reshape(3 * ch, half)
            total[c] += jnp.dot(window, part, preferred_element_type=jnp.float32)


def store(total, out):
    half = total.shape[-1]
    for c in range(2):
        out[:, :, c * half : (c + 1) * half] = total[c].astype(jnp.bfloat16).reshape(ROWS, LINE, half)


def near_kernel(step, where, cells, *refs):
    weights, (out, shifted, kernel, total, sems) = refs[:4], refs[4:]
    groups = weight_copies(False, where, weights, kernel, sems)
    for copy in sum(groups, []):
        copy.start()
    convolve(step, cells, groups, shifted, kernel, total)
    store(total, out)


def far_kernel(step, where, cells, *refs):
    pieces, (out, shifted, kernel, total, up_rows, down_rows, sems, mlp_sems) = refs[:8], refs[8:]
    ch = cells.shape[-1]
    half = ch // 2
    groups = weight_copies(True, where, pieces, kernel, sems)
    for copy in sum(groups, []):
        copy.start()
    mlp = []
    for n, piece in enumerate(pieces):
        mlp.append([])
        for c in range(2):
            for kind, rows in enumerate((up_rows, down_rows)):
                blocks = piece.at[:, pl.ds(TAPS + 4 * c + 2 * kind, 2)]
                place = rows.at[n, :, :, :, :, pl.ds(c * half, half)]
                mlp[n].append(pltpu.make_async_copy(blocks, place, mlp_sems.at[n * 4 + 2 * c + kind]))
    for copy in sum(mlp, []):
        copy.start()
    convolve(step, cells, groups, shifted, kernel, total)
    squares = 0.0
    for c in range(2):
        value = total[c].astype(jnp.bfloat16).astype(jnp.float32)
        total[c] = value
        squares = squares + jnp.sum(value * value, axis=-1, keepdims=True)
    scale = lax.rsqrt(squares / ch + 1e-06)
    rows = jnp.concatenate([(total[c] * scale).astype(jnp.bfloat16) for c in range(2)], axis=1)
    for n in range(0, 8, 2):
        for copy in mlp[n] + mlp[n + 1]:
            copy.wait()
        up = up_rows[n : n + 2].reshape(-1, ch)
        down = down_rows[n : n + 2].reshape(-1, ch)
        hidden = lax.dot_general(rows, up, (((1,), (1,)), ((), ())), preferred_element_type=jnp.float32)
        hidden = jax.nn.gelu(hidden).astype(jnp.bfloat16)
        for c in range(2):
            total[c] += jnp.dot(hidden, down[:, c * half : (c + 1) * half], preferred_element_type=jnp.float32)
    store(total, out)


def block(kernel, cells, weights, step, where, mlp):
    ch = cells.shape[-1]
    whole = pl.BlockSpec(memory_space=pltpu.VMEM)
    scratch = [
        pltpu.VMEM((ROWS + 2 * step, LINE, 3 * ch), jnp.bfloat16),
        pltpu.VMEM((2, TAPS, 2, 8, 4, 8, ch // 2), jnp.bfloat16),
        pltpu.VMEM((2, CELLS, ch // 2), jnp.float32),
    ]
    semaphores = [pltpu.SemaphoreType.DMA((48,))]
    if mlp:
        scratch += [pltpu.VMEM((8, 2, 2, 8, 8, ch), jnp.bfloat16)] * 2
        semaphores += [pltpu.SemaphoreType.DMA((32,))]
    return pl.pallas_call(
        functools.partial(kernel, step),
        out_shape=jax.ShapeDtypeStruct(cells.shape, jnp.bfloat16),
        in_specs=[pl.BlockSpec(memory_space=pltpu.SMEM), whole] + [pl.BlockSpec(memory_space=pl.ANY)] * len(weights),
        out_specs=whole,
        scratch_shapes=scratch + semaphores,
        compiler_params=pltpu.CompilerParams(vmem_limit_bytes=VMEM_LIMIT),
        cost_estimate=pl.CostEstimate(flops=1000, bytes_accessed=1000, transcendentals=0),
    )(where, cells, *weights)


def shards(inputs, tight, wide, up, down):
    core = lax.axis_index("core")
    where = jnp.stack([lax.axis_index("x"), lax.axis_index("ylo"), core]).astype(jnp.int32)
    s, i, cols, ch = inputs.shape
    half, n = ch // 2, down.shape[0] // 2
    kernels = jnp.concatenate([tight.reshape(TAPS, 8, ch), wide.reshape(TAPS, 8, ch)])
    kernels = lax.dynamic_slice_in_dim(kernels, core * half, half, axis=2)
    mlp = jnp.stack([lax.dynamic_slice_in_dim(up.T, core * n, n, 0), lax.dynamic_slice_in_dim(down, core * n, n, 0)])
    mlp = jnp.stack([mlp[:, :, :half], mlp[:, :, half:]]).reshape(MLP, 8, half)
    shard = jnp.concatenate([kernels, mlp])

    cells = inputs.reshape(s, i, 8, 8, PAIR, ch).transpose(0, 1, 3, 2, 4, 5).reshape(64, 16, ch)
    shard = shard.reshape(-1, 1, 8, half)
    for bit in (2, 1, 0):
        shard = joined(shard, from_z(shard, bit), (lax.axis_index("z") >> bit) & 1)
    shard = shard.reshape(-1, 8, 8, half)
    shard, cells = lax.optimization_barrier((shard, cells))
    cells = lax.all_to_all(cells, PEERS, 0, 0).reshape(ROWS, LINE, ch)

    near_half = jnp.stack([shard[:TAPS], from_y(shard[:TAPS])])
    rest = shard[TAPS:]
    first = jnp.stack([rest, from_x(rest, 0)])
    second = from_x(first, 1)
    first_y = from_y(first)
    t_first = jnp.stack([near_half, from_x(near_half, 0)])
    t_second = from_x(t_first, 1)
    t_second, cells = lax.optimization_barrier((t_second, cells))
    tight_parts = [t_first, t_second, from_core(t_first), from_core(t_second)]
    second, first_y = lax.optimization_barrier((second, first_y))
    own = [first, second, first_y, from_y(second)]
    parts = own + [from_core(piece) for piece in own]

    near = block(near_kernel, cells, tight_parts, 1, where, False)
    out = block(far_kernel, near, parts, 4, where, True)
    out = lax.all_to_all(out.reshape(64, 16, ch), PEERS, 0, 0)
    return out.reshape(s, i, 8, 8, PAIR, ch).transpose(0, 1, 3, 2, 4, 5).reshape(inputs.shape)


def solution(mesh):
    grid = Mesh(mesh.devices.reshape(SIZES), AXES)
    rows, columns = ("ylo", "z", "x"), ("yhi", "core")
    placed = (
        P(None, rows, columns, None),
        P(None, None, rows, None),
        P(None, None, rows, None),
        P(None, rows),
        P(rows, None),
    )
    return jax.shard_map(shards, mesh=grid, in_specs=placed, out_specs=P(None, rows, columns, None), check_vma=False)
```

```python
import functools

import jax
import jax.numpy as jnp
import numpy as np
from jax import lax
from jax.experimental import pallas as pl
from jax.experimental.pallas import tpu as pltpu
from jax.sharding import Mesh, PartitionSpec as P

AXES = ("ylo", "z", "x", "yhi", "core")
SIZES = (2, 8, 4, 2, 2)
PEERS = ("ylo", "z", "yhi", "core")
ROWS, COLS, PAIR = 16, 32, 2
LINE = COLS * PAIR
CELLS = ROWS * LINE
TAPS = 9
MLP = 8
VMEM_LIMIT = 56 * 1024 * 1024


def moved(array, to):
    pairs = []
    for source, (ylo, z, x, yhi, core) in enumerate(np.ndindex(SIZES)):
        y, z, x, core = to(2 * yhi + ylo, z, x, core)
        y, z, x, core = y % 4, z % 8, x % 4, core % 2
        pairs.append((source, int(np.ravel_multi_index((y % 2, z, x, y // 2, core), SIZES))))
    return lax.ppermute(array, AXES, pairs)


def from_x(piece, turn):
    return moved(piece, lambda y, z, x, c: (y, z, x ^ (3 if c != turn else 1), c))


def from_z(piece):
    def partner(y, z, x, c):
        return y, z + (1 if (z + c) % 2 == 0 else -1), x, c

    return moved(piece, partner)


def joined(mine, theirs, place):
    pair = [jnp.where(place == 0, mine, theirs), jnp.where(place == 0, theirs, mine)]
    n, pieces, rows, width = mine.shape
    return jnp.stack(pair, axis=2).reshape(n, 2 * pieces, rows, width)


def from_y(piece):
    return moved(piece, lambda y, z, x, c: (y + 1 - 2 * c, z, x, c))


def from_core(piece):
    return moved(piece, lambda y, z, x, c: (y, z, x, 1 - c))


def x_slots(x, core):
    first = jnp.where(core == 0, x ^ 1, x ^ 3)
    return x, first, x ^ first ^ (x ^ 2), x ^ 2


def normalized(values):
    return values * lax.rsqrt(jnp.mean(values * values, axis=-1, keepdims=True) + 1e-06)


def weight_copies(split_y, where, sources, kernel, sems):
    x, ylo, core = where[0], where[1], where[2]
    groups = [[], [], []]
    for i in range(3):
        taps = pl.ds(3 * i, 3)
        for far in range(2):
            c = core if far == 0 else 1 - core
            slots = x_slots(x, c)
            for y in range(2):
                y_of = ylo if y == 0 else 1 - ylo
                for part in range(2):
                    for k in range(2):
                        if split_y:
                            source = sources[far * 4 + y * 2 + part].at[k, taps]
                        else:
                            source = sources[far * 2 + part].at[k, y, taps]
                        place = kernel.at[c, taps, y_of, :, slots[part * 2 + k]]
                        groups[i].append(pltpu.make_async_copy(source, place, sems.at[i * 16 + len(groups[i])]))
    return groups


def convolve(step, cells, groups, shifted, kernel, total):
    ch = cells.shape[-1]
    half = ch // 2
    blank = jnp.zeros((step, LINE, 3 * ch), jnp.bfloat16)
    shifted[pl.ds(0, step)] = blank
    shifted[pl.ds(ROWS + step, step)] = blank
    by = step * PAIR

    def fill(r, _):
        raw = cells[r].astype(jnp.float32)
        for c in range(2):
            total[c, pl.ds(pl.multiple_of(r * LINE, LINE), LINE)] = raw[:, c * half : (c + 1) * half]
        row = normalized(raw)
        edge = jnp.zeros((by, ch), jnp.float32)
        if by % 8 == 0:
            before = jnp.concatenate([edge, row[: LINE - by]], axis=0)
            after = jnp.concatenate([row[by:], edge], axis=0)
        else:
            column = lax.broadcasted_iota(jnp.int32, (LINE, ch), 0)
            before = jnp.where(column >= by, pltpu.roll(row, by, 0), 0.0)
            after = jnp.where(column < LINE - by, pltpu.roll(row, LINE - by, 0), 0.0)
        for j, values in enumerate((before, row, after)):
            shifted[r + step, :, j * ch : (j + 1) * ch] = values.astype(jnp.bfloat16)
        return 0

    lax.fori_loop(0, ROWS, fill, 0, unroll=2)
    for i in range(3):
        for copy in groups[i]:
            copy.wait()
        window = shifted[pl.ds(i * step, ROWS)].reshape(CELLS, 3 * ch)
        for c in range(2):
            part = kernel[c, pl.ds(3 * i, 3)].reshape(3 * ch, half)
            total[c] += jnp.dot(window, part, preferred_element_type=jnp.float32)


def store(total, out):
    half = total.shape[-1]
    for c in range(2):
        out[:, :, c * half : (c + 1) * half] = total[c].astype(jnp.bfloat16).reshape(ROWS, LINE, half)


def near_kernel(step, where, cells, *refs):
    weights, (out, shifted, kernel, total, sems) = refs[:4], refs[4:]
    groups = weight_copies(False, where, weights, kernel, sems)
    for copy in sum(groups, []):
        copy.start()
    convolve(step, cells, groups, shifted, kernel, total)
    store(total, out)


def far_kernel(step, where, cells, *refs):
    pieces, (out, shifted, kernel, total, up_rows, down_rows, sems, mlp_sems) = refs[:8], refs[8:]
    ch = cells.shape[-1]
    half = ch // 2
    groups = weight_copies(True, where, pieces, kernel, sems)
    for copy in sum(groups, []):
        copy.start()
    mlp = []
    for n, piece in enumerate(pieces):
        mlp.append([])
        for c in range(2):
            for kind, rows in enumerate((up_rows, down_rows)):
                blocks = piece.at[:, pl.ds(TAPS + 4 * c + 2 * kind, 2)]
                place = rows.at[n, :, :, :, :, pl.ds(c * half, half)]
                mlp[n].append(pltpu.make_async_copy(blocks, place, mlp_sems.at[n * 4 + 2 * c + kind]))
    for copy in sum(mlp, []):
        copy.start()
    convolve(step, cells, groups, shifted, kernel, total)
    squares = 0.0
    for c in range(2):
        value = total[c].astype(jnp.bfloat16).astype(jnp.float32)
        total[c] = value
        squares = squares + jnp.sum(value * value, axis=-1, keepdims=True)
    scale = lax.rsqrt(squares / ch + 1e-06)
    rows = jnp.concatenate([(total[c] * scale).astype(jnp.bfloat16) for c in range(2)], axis=1)
    for n in range(0, 8, 2):
        for copy in mlp[n] + mlp[n + 1]:
            copy.wait()
        up = up_rows[n : n + 2].reshape(-1, ch)
        down = down_rows[n : n + 2].reshape(-1, ch)
        hidden = lax.dot_general(rows, up, (((1,), (1,)), ((), ())), preferred_element_type=jnp.float32)
        hidden = jax.nn.gelu(hidden).astype(jnp.bfloat16)
        for c in range(2):
            total[c] += jnp.dot(hidden, down[:, c * half : (c + 1) * half], preferred_element_type=jnp.float32)
    store(total, out)


def block(kernel, cells, weights, step, where, mlp):
    ch = cells.shape[-1]
    whole = pl.BlockSpec(memory_space=pltpu.VMEM)
    scratch = [
        pltpu.VMEM((ROWS + 2 * step, LINE, 3 * ch), jnp.bfloat16),
        pltpu.VMEM((2, TAPS, 2, 8, 4, 8, ch // 2), jnp.bfloat16),
        pltpu.VMEM((2, CELLS, ch // 2), jnp.float32),
    ]
    semaphores = [pltpu.SemaphoreType.DMA((48,))]
    if mlp:
        scratch += [pltpu.VMEM((8, 2, 2, 8, 8, ch), jnp.bfloat16)] * 2
        semaphores += [pltpu.SemaphoreType.DMA((32,))]
    return pl.pallas_call(
        functools.partial(kernel, step),
        out_shape=jax.ShapeDtypeStruct(cells.shape, jnp.bfloat16),
        in_specs=[pl.BlockSpec(memory_space=pltpu.SMEM), whole] + [pl.BlockSpec(memory_space=pl.ANY)] * len(weights),
        out_specs=whole,
        scratch_shapes=scratch + semaphores,
        compiler_params=pltpu.CompilerParams(vmem_limit_bytes=VMEM_LIMIT),
        cost_estimate=pl.CostEstimate(flops=1000, bytes_accessed=1000, transcendentals=0),
    )(where, cells, *weights)


def shards(inputs, tight, wide, up, down):
    core = lax.axis_index("core")
    where = jnp.stack([lax.axis_index("x"), lax.axis_index("ylo"), core]).astype(jnp.int32)
    s, i, cols, ch = inputs.shape
    half, n = ch // 2, down.shape[0] // 2
    kernels = jnp.concatenate([tight.reshape(TAPS, 8, ch), wide.reshape(TAPS, 8, ch)])
    kernels = lax.dynamic_slice_in_dim(kernels, core * half, half, axis=2)
    mlp = jnp.stack([lax.dynamic_slice_in_dim(up.T, core * n, n, 0), lax.dynamic_slice_in_dim(down, core * n, n, 0)])
    mlp = jnp.stack([mlp[:, :, :half], mlp[:, :, half:]]).reshape(MLP, 8, half)
    shard = jnp.concatenate([kernels, mlp])

    cells = inputs.reshape(s, i, 8, 8, PAIR, ch).transpose(0, 1, 3, 2, 4, 5).reshape(64, 16, ch)
    shard = shard.reshape(-1, 1, 8, half)
    quarters = [shard] + [moved(shard, lambda y, z, x, c, k=k: (y, z ^ k, x, c)) for k in (2, 4, 6)]
    for bit in (0, 1):
        turned = (lax.axis_index("z") >> (bit + 1)) & 1 == 1
        quarters = [jnp.where(turned, quarters[q ^ (1 << bit)], quarters[q]) for q in range(4)]
    shard = jnp.concatenate(quarters, axis=1)
    shard = joined(shard, from_z(shard), lax.axis_index("z") & 1)
    shard = shard.reshape(-1, 8, 8, half)
    shard, cells = lax.optimization_barrier((shard, cells))
    cells = lax.all_to_all(cells, PEERS, 0, 0).reshape(ROWS, LINE, ch)

    near_half = jnp.stack([shard[:TAPS], from_y(shard[:TAPS])])
    rest = shard[TAPS:]
    first = jnp.stack([rest, from_x(rest, 0)])
    second = from_x(first, 1)
    first_y = from_y(first)
    t_first = jnp.stack([near_half, from_x(near_half, 0)])
    t_second = from_x(t_first, 1)
    t_second, cells = lax.optimization_barrier((t_second, cells))
    tight_parts = [t_first, t_second, from_core(t_first), from_core(t_second)]
    second, first_y = lax.optimization_barrier((second, first_y))
    own = [first, second, first_y, from_y(second)]
    parts = own + [from_core(piece) for piece in own]

    near = block(near_kernel, cells, tight_parts, 1, where, False)
    out = block(far_kernel, near, parts, 4, where, True)
    out = lax.all_to_all(out.reshape(64, 16, ch), PEERS, 0, 0)
    return out.reshape(s, i, 8, 8, PAIR, ch).transpose(0, 1, 3, 2, 4, 5).reshape(inputs.shape)


def solution(mesh):
    grid = Mesh(mesh.devices.reshape(SIZES), AXES)
    rows, columns = ("ylo", "z", "x"), ("yhi", "core")
    placed = (
        P(None, rows, columns, None),
        P(None, None, rows, None),
        P(None, None, rows, None),
        P(None, rows),
        P(rows, None),
    )
    return jax.shard_map(shards, mesh=grid, in_specs=placed, out_specs=P(None, rows, columns, None), check_vma=False)
```

```python
import functools

import jax
import jax.numpy as jnp
import numpy as np
from jax import lax
from jax.experimental import pallas as pl
from jax.experimental.pallas import tpu as pltpu
from jax.sharding import Mesh, PartitionSpec as P

AXES = ("ylo", "z", "x", "yhi", "core")
SIZES = (2, 8, 4, 2, 2)
PEERS = ("ylo", "z", "yhi", "core")
ROWS, COLS, PAIR = 16, 32, 2
LINE = COLS * PAIR
CELLS = ROWS * LINE
TAPS = 9
MLP = 8
VMEM_LIMIT = 56 * 1024 * 1024


def moved(array, to):
    pairs = []
    for source, (ylo, z, x, yhi, core) in enumerate(np.ndindex(SIZES)):
        y, z, x, core = to(2 * yhi + ylo, z, x, core)
        y, z, x, core = y % 4, z % 8, x % 4, core % 2
        pairs.append((source, int(np.ravel_multi_index((y % 2, z, x, y // 2, core), SIZES))))
    return lax.ppermute(array, AXES, pairs)


def from_x(piece, turn):
    return moved(piece, lambda y, z, x, c: (y, z, x ^ (3 if c != turn else 1), c))


def from_z(piece):
    def partner(y, z, x, c):
        return y, z + (1 if (z + c) % 2 == 0 else -1), x, c

    return moved(piece, partner)


def joined(mine, theirs, place):
    pair = [jnp.where(place == 0, mine, theirs), jnp.where(place == 0, theirs, mine)]
    n, pieces, rows, width = mine.shape
    return jnp.stack(pair, axis=2).reshape(n, 2 * pieces, rows, width)


def from_y(piece):
    return moved(piece, lambda y, z, x, c: (y + 1 - 2 * c, z, x, c))


def from_core(piece):
    return moved(piece, lambda y, z, x, c: (y, z, x, 1 - c))


def x_slots(x, core):
    first = jnp.where(core == 0, x ^ 1, x ^ 3)
    return x, first, x ^ first ^ (x ^ 2), x ^ 2


def normalized(values):
    return values * lax.rsqrt(jnp.mean(values * values, axis=-1, keepdims=True) + 1e-06)


def weight_copies(split_y, where, sources, kernel, sems):
    x, ylo, core = where[0], where[1], where[2]
    groups = [[], [], []]
    for i in range(3):
        taps = pl.ds(3 * i, 3)
        for far in range(2):
            c = core if far == 0 else 1 - core
            slots = x_slots(x, c)
            for y in range(2):
                y_of = ylo if y == 0 else 1 - ylo
                for part in range(2):
                    for k in range(2):
                        if split_y:
                            source = sources[far * 4 + y * 2 + part].at[k, taps]
                        else:
                            source = sources[far * 2 + part].at[k, y, taps]
                        place = kernel.at[c, taps, y_of, :, slots[part * 2 + k]]
                        groups[i].append(pltpu.make_async_copy(source, place, sems.at[i * 16 + len(groups[i])]))
    return groups


def convolve(step, cells, groups, shifted, kernel, total):
    ch = cells.shape[-1]
    half = ch // 2
    blank = jnp.zeros((step, LINE, 3 * ch), jnp.bfloat16)
    shifted[pl.ds(0, step)] = blank
    shifted[pl.ds(ROWS + step, step)] = blank
    by = step * PAIR

    def fill(r, _):
        raw = cells[r].astype(jnp.float32)
        for c in range(2):
            total[c, pl.ds(pl.multiple_of(r * LINE, LINE), LINE)] = raw[:, c * half : (c + 1) * half]
        row = normalized(raw)
        edge = jnp.zeros((by, ch), jnp.float32)
        if by % 8 == 0:
            before = jnp.concatenate([edge, row[: LINE - by]], axis=0)
            after = jnp.concatenate([row[by:], edge], axis=0)
        else:
            column = lax.broadcasted_iota(jnp.int32, (LINE, ch), 0)
            before = jnp.where(column >= by, pltpu.roll(row, by, 0), 0.0)
            after = jnp.where(column < LINE - by, pltpu.roll(row, LINE - by, 0), 0.0)
        for j, values in enumerate((before, row, after)):
            shifted[r + step, :, j * ch : (j + 1) * ch] = values.astype(jnp.bfloat16)
        return 0

    lax.fori_loop(0, ROWS, fill, 0, unroll=2)
    for i in range(3):
        for copy in groups[i]:
            copy.wait()
        window = shifted[pl.ds(i * step, ROWS)].reshape(CELLS, 3 * ch)
        for c in range(2):
            part = kernel[c, pl.ds(3 * i, 3)].reshape(3 * ch, half)
            total[c] += jnp.dot(window, part, preferred_element_type=jnp.float32)


def store(total, out):
    half = total.shape[-1]
    for c in range(2):
        out[:, :, c * half : (c + 1) * half] = total[c].astype(jnp.bfloat16).reshape(ROWS, LINE, half)


def near_kernel(step, where, cells, *refs):
    weights, (out, shifted, kernel, total, sems) = refs[:4], refs[4:]
    groups = weight_copies(False, where, weights, kernel, sems)
    for copy in sum(groups, []):
        copy.start()
    convolve(step, cells, groups, shifted, kernel, total)
    store(total, out)


def far_kernel(step, where, cells, *refs):
    pieces, (out, shifted, kernel, total, up_rows, down_rows, sems, mlp_sems) = refs[:8], refs[8:]
    ch = cells.shape[-1]
    half = ch // 2
    groups = weight_copies(True, where, pieces, kernel, sems)
    for copy in sum(groups, []):
        copy.start()
    mlp = []
    for n, piece in enumerate(pieces):
        mlp.append([])
        for c in range(2):
            for kind, rows in enumerate((up_rows, down_rows)):
                blocks = piece.at[:, pl.ds(TAPS + 4 * c + 2 * kind, 2)]
                place = rows.at[n, :, :, :, :, pl.ds(c * half, half)]
                mlp[n].append(pltpu.make_async_copy(blocks, place, mlp_sems.at[n * 4 + 2 * c + kind]))
    for copy in sum(mlp, []):
        copy.start()
    convolve(step, cells, groups, shifted, kernel, total)
    squares = 0.0
    for c in range(2):
        value = total[c].astype(jnp.bfloat16).astype(jnp.float32)
        total[c] = value
        squares = squares + jnp.sum(value * value, axis=-1, keepdims=True)
    scale = lax.rsqrt(squares / ch + 1e-06)
    rows = jnp.concatenate([(total[c] * scale).astype(jnp.bfloat16) for c in range(2)], axis=1)
    for n in range(0, 8, 2):
        for copy in mlp[n] + mlp[n + 1]:
            copy.wait()
        up = up_rows[n : n + 2].reshape(-1, ch)
        down = down_rows[n : n + 2].reshape(-1, ch)
        hidden = lax.dot_general(rows, up, (((1,), (1,)), ((), ())), preferred_element_type=jnp.float32)
        hidden = jax.nn.gelu(hidden).astype(jnp.bfloat16)
        for c in range(2):
            total[c] += jnp.dot(hidden, down[:, c * half : (c + 1) * half], preferred_element_type=jnp.float32)
    store(total, out)


def block(kernel, cells, weights, step, where, mlp):
    ch = cells.shape[-1]
    whole = pl.BlockSpec(memory_space=pltpu.VMEM)
    scratch = [
        pltpu.VMEM((ROWS + 2 * step, LINE, 3 * ch), jnp.bfloat16),
        pltpu.VMEM((2, TAPS, 2, 8, 4, 8, ch // 2), jnp.bfloat16),
        pltpu.VMEM((2, CELLS, ch // 2), jnp.float32),
    ]
    semaphores = [pltpu.SemaphoreType.DMA((48,))]
    if mlp:
        scratch += [pltpu.VMEM((8, 2, 2, 8, 8, ch), jnp.bfloat16)] * 2
        semaphores += [pltpu.SemaphoreType.DMA((32,))]
    return pl.pallas_call(
        functools.partial(kernel, step),
        out_shape=jax.ShapeDtypeStruct(cells.shape, jnp.bfloat16),
        in_specs=[pl.BlockSpec(memory_space=pltpu.SMEM), whole] + [pl.BlockSpec(memory_space=pl.ANY)] * len(weights),
        out_specs=whole,
        scratch_shapes=scratch + semaphores,
        compiler_params=pltpu.CompilerParams(vmem_limit_bytes=VMEM_LIMIT),
        cost_estimate=pl.CostEstimate(flops=1000, bytes_accessed=1000, transcendentals=0),
    )(where, cells, *weights)


def shards(inputs, tight, wide, up, down):
    core = lax.axis_index("core")
    where = jnp.stack([lax.axis_index("x"), lax.axis_index("ylo"), core]).astype(jnp.int32)
    s, i, cols, ch = inputs.shape
    half, n = ch // 2, down.shape[0] // 2
    kernels = jnp.concatenate([tight.reshape(TAPS, 8, ch), wide.reshape(TAPS, 8, ch)])
    kernels = lax.dynamic_slice_in_dim(kernels, core * half, half, axis=2)
    mlp = jnp.stack([lax.dynamic_slice_in_dim(up.T, core * n, n, 0), lax.dynamic_slice_in_dim(down, core * n, n, 0)])
    mlp = jnp.stack([mlp[:, :, :half], mlp[:, :, half:]]).reshape(MLP, 8, half)
    shard = jnp.concatenate([kernels, mlp])

    cells = inputs.reshape(s, i, 8, 8, PAIR, ch).transpose(0, 1, 3, 2, 4, 5).reshape(64, 16, ch)
    shard = shard.reshape(-1, 1, 8, half)
    quarters = [shard] + [moved(shard, lambda y, z, x, c, k=k: (y, z ^ k, x, c)) for k in (2, 4, 6)]
    for bit in (0, 1):
        turned = (lax.axis_index("z") >> (bit + 1)) & 1 == 1
        quarters = [jnp.where(turned, quarters[q ^ (1 << bit)], quarters[q]) for q in range(4)]
    shard = jnp.concatenate(quarters, axis=1)
    shard = joined(shard, from_z(shard), lax.axis_index("z") & 1)
    shard = shard.reshape(-1, 8, 8, half)
    shard, cells = lax.optimization_barrier((shard, cells))
    cells = lax.all_to_all(cells, PEERS, 0, 0).reshape(ROWS, LINE, ch)

    near_half = jnp.stack([shard[:TAPS], from_y(shard[:TAPS])])
    rest = shard[TAPS:]
    first = jnp.stack([rest, from_x(rest, 0)])
    second = from_x(first, 1)
    first_y = from_y(first)
    t_first = jnp.stack([near_half, from_x(near_half, 0)])
    t_second = from_x(t_first, 1)
    tight_parts = [t_first, t_second, from_core(t_first), from_core(t_second)]
    second, first_y = lax.optimization_barrier((second, first_y))
    own = [first, second, first_y, from_y(second)]
    late, cells = lax.optimization_barrier((own[2], cells))
    parts = own + [from_core(late if n == 2 else piece) for n, piece in enumerate(own)]

    near = block(near_kernel, cells, tight_parts, 1, where, False)
    out = block(far_kernel, near, parts, 4, where, True)
    out = lax.all_to_all(out.reshape(64, 16, ch), PEERS, 0, 0)
    return out.reshape(s, i, 8, 8, PAIR, ch).transpose(0, 1, 3, 2, 4, 5).reshape(inputs.shape)


def solution(mesh):
    grid = Mesh(mesh.devices.reshape(SIZES), AXES)
    rows, columns = ("ylo", "z", "x"), ("yhi", "core")
    placed = (
        P(None, rows, columns, None),
        P(None, None, rows, None),
        P(None, None, rows, None),
        P(None, rows),
        P(rows, None),
    )
    return jax.shard_map(shards, mesh=grid, in_specs=placed, out_specs=P(None, rows, columns, None), check_vma=False)
```

```python
import functools

import jax
import jax.numpy as jnp
import numpy as np
from jax import lax
from jax.experimental import pallas as pl
from jax.experimental.pallas import tpu as pltpu
from jax.sharding import Mesh, PartitionSpec as P

AXES = ("ylo", "z", "x", "yhi", "core")
SIZES = (2, 8, 4, 2, 2)
PEERS = ("ylo", "z", "yhi", "core")
ROWS, COLS, PAIR = 16, 32, 2
LINE = COLS * PAIR
CELLS = ROWS * LINE
TAPS = 9
MLP = 8
VMEM_LIMIT = 56 * 1024 * 1024


def moved(array, to):
    pairs = []
    for source, (ylo, z, x, yhi, core) in enumerate(np.ndindex(SIZES)):
        y, z, x, core = to(2 * yhi + ylo, z, x, core)
        y, z, x, core = y % 4, z % 8, x % 4, core % 2
        pairs.append((source, int(np.ravel_multi_index((y % 2, z, x, y // 2, core), SIZES))))
    return lax.ppermute(array, AXES, pairs)


def from_x(piece, turn):
    return moved(piece, lambda y, z, x, c: (y, z, x ^ (3 if c != turn else 1), c))


def from_z(piece):
    def partner(y, z, x, c):
        return y, z + (1 if (z + c) % 2 == 0 else -1), x, c

    return moved(piece, partner)


def joined(mine, theirs, place):
    pair = [jnp.where(place == 0, mine, theirs), jnp.where(place == 0, theirs, mine)]
    n, pieces, rows, width = mine.shape
    return jnp.stack(pair, axis=2).reshape(n, 2 * pieces, rows, width)


def from_y(piece):
    return moved(piece, lambda y, z, x, c: (y + 1 - 2 * c, z, x, c))


def from_core(piece):
    return moved(piece, lambda y, z, x, c: (y, z, x, 1 - c))


def x_slots(x, core):
    first = jnp.where(core == 0, x ^ 1, x ^ 3)
    return x, first, x ^ first ^ (x ^ 2), x ^ 2


def normalized(values):
    return values * lax.rsqrt(jnp.mean(values * values, axis=-1, keepdims=True) + 1e-06)


def weight_copies(split_y, where, sources, kernel, sems):
    x, ylo, core = where[0], where[1], where[2]
    groups = [[], [], []]
    for i in range(3):
        taps = pl.ds(3 * i, 3)
        for far in range(2):
            c = core if far == 0 else 1 - core
            slots = x_slots(x, c)
            for y in range(2):
                y_of = ylo if y == 0 else 1 - ylo
                for part in range(2):
                    for k in range(2):
                        if split_y:
                            source = sources[far * 4 + y * 2 + part].at[k, taps]
                        else:
                            source = sources[far * 2 + part].at[k, y, taps]
                        place = kernel.at[c, taps, y_of, :, slots[part * 2 + k]]
                        groups[i].append(pltpu.make_async_copy(source, place, sems.at[i * 16 + len(groups[i])]))
    return groups


def convolve(step, cells, groups, shifted, kernel, total):
    ch = cells.shape[-1]
    half = ch // 2
    blank = jnp.zeros((step, LINE, 3 * ch), jnp.bfloat16)
    shifted[pl.ds(0, step)] = blank
    shifted[pl.ds(ROWS + step, step)] = blank
    by = step * PAIR

    def fill(r, _):
        raw = cells[r].astype(jnp.float32)
        for c in range(2):
            total[c, pl.ds(pl.multiple_of(r * LINE, LINE), LINE)] = raw[:, c * half : (c + 1) * half]
        row = normalized(raw)
        edge = jnp.zeros((by, ch), jnp.float32)
        if by % 8 == 0:
            before = jnp.concatenate([edge, row[: LINE - by]], axis=0)
            after = jnp.concatenate([row[by:], edge], axis=0)
        else:
            column = lax.broadcasted_iota(jnp.int32, (LINE, ch), 0)
            before = jnp.where(column >= by, pltpu.roll(row, by, 0), 0.0)
            after = jnp.where(column < LINE - by, pltpu.roll(row, LINE - by, 0), 0.0)
        for j, values in enumerate((before, row, after)):
            shifted[r + step, :, j * ch : (j + 1) * ch] = values.astype(jnp.bfloat16)
        return 0

    lax.fori_loop(0, ROWS, fill, 0, unroll=2)
    for i in range(3):
        for copy in groups[i]:
            copy.wait()
        window = shifted[pl.ds(i * step, ROWS)].reshape(CELLS, 3 * ch)
        for c in range(2):
            part = kernel[c, pl.ds(3 * i, 3)].reshape(3 * ch, half)
            total[c] += jnp.dot(window, part, preferred_element_type=jnp.float32)


def store(total, out):
    half = total.shape[-1]
    for c in range(2):
        out[:, :, c * half : (c + 1) * half] = total[c].astype(jnp.bfloat16).reshape(ROWS, LINE, half)


def near_kernel(step, where, cells, *refs):
    weights, (out, shifted, kernel, total, sems) = refs[:4], refs[4:]
    groups = weight_copies(False, where, weights, kernel, sems)
    for copy in sum(groups, []):
        copy.start()
    convolve(step, cells, groups, shifted, kernel, total)
    store(total, out)


def far_kernel(step, where, cells, *refs):
    pieces, (out, shifted, kernel, total, up_rows, down_rows, sems, mlp_sems) = refs[:8], refs[8:]
    ch = cells.shape[-1]
    half = ch // 2
    groups = weight_copies(True, where, pieces, kernel, sems)
    for copy in sum(groups, []):
        copy.start()
    mlp = []
    for n, piece in enumerate(pieces):
        mlp.append([])
        for c in range(2):
            for kind, rows in enumerate((up_rows, down_rows)):
                blocks = piece.at[:, pl.ds(TAPS + 4 * c + 2 * kind, 2)]
                place = rows.at[n, :, :, :, :, pl.ds(c * half, half)]
                mlp[n].append(pltpu.make_async_copy(blocks, place, mlp_sems.at[n * 4 + 2 * c + kind]))
    for copy in sum(mlp, []):
        copy.start()
    convolve(step, cells, groups, shifted, kernel, total)
    squares = 0.0
    for c in range(2):
        value = total[c].astype(jnp.bfloat16).astype(jnp.float32)
        total[c] = value
        squares = squares + jnp.sum(value * value, axis=-1, keepdims=True)
    scale = lax.rsqrt(squares / ch + 1e-06)
    rows = jnp.concatenate([(total[c] * scale).astype(jnp.bfloat16) for c in range(2)], axis=1)
    for n in range(0, 8, 2):
        for copy in mlp[n] + mlp[n + 1]:
            copy.wait()
        up = up_rows[n : n + 2].reshape(-1, ch)
        down = down_rows[n : n + 2].reshape(-1, ch)
        hidden = lax.dot_general(rows, up, (((1,), (1,)), ((), ())), preferred_element_type=jnp.float32)
        hidden = jax.nn.gelu(hidden).astype(jnp.bfloat16)
        for c in range(2):
            total[c] += jnp.dot(hidden, down[:, c * half : (c + 1) * half], preferred_element_type=jnp.float32)
    store(total, out)


def block(kernel, cells, weights, step, where, mlp):
    ch = cells.shape[-1]
    whole = pl.BlockSpec(memory_space=pltpu.VMEM)
    scratch = [
        pltpu.VMEM((ROWS + 2 * step, LINE, 3 * ch), jnp.bfloat16),
        pltpu.VMEM((2, TAPS, 2, 8, 4, 8, ch // 2), jnp.bfloat16),
        pltpu.VMEM((2, CELLS, ch // 2), jnp.float32),
    ]
    semaphores = [pltpu.SemaphoreType.DMA((48,))]
    if mlp:
        scratch += [pltpu.VMEM((8, 2, 2, 8, 8, ch), jnp.bfloat16)] * 2
        semaphores += [pltpu.SemaphoreType.DMA((32,))]
    return pl.pallas_call(
        functools.partial(kernel, step),
        out_shape=jax.ShapeDtypeStruct(cells.shape, jnp.bfloat16),
        in_specs=[pl.BlockSpec(memory_space=pltpu.SMEM), whole] + [pl.BlockSpec(memory_space=pl.ANY)] * len(weights),
        out_specs=whole,
        scratch_shapes=scratch + semaphores,
        compiler_params=pltpu.CompilerParams(vmem_limit_bytes=VMEM_LIMIT),
        cost_estimate=pl.CostEstimate(flops=1000, bytes_accessed=1000, transcendentals=0),
    )(where, cells, *weights)


def shards(inputs, tight, wide, up, down):
    core = lax.axis_index("core")
    where = jnp.stack([lax.axis_index("x"), lax.axis_index("ylo"), core]).astype(jnp.int32)
    s, i, cols, ch = inputs.shape
    half, n = ch // 2, down.shape[0] // 2
    kernels = jnp.concatenate([tight.reshape(TAPS, 8, ch), wide.reshape(TAPS, 8, ch)])
    kernels = lax.dynamic_slice_in_dim(kernels, core * half, half, axis=2)
    mlp = jnp.stack([lax.dynamic_slice_in_dim(up.T, core * n, n, 0), lax.dynamic_slice_in_dim(down, core * n, n, 0)])
    mlp = jnp.stack([mlp[:, :, :half], mlp[:, :, half:]]).reshape(MLP, 8, half)
    shard = jnp.concatenate([kernels, mlp])

    cells = inputs.reshape(s, i, 8, 8, PAIR, ch).transpose(0, 1, 3, 2, 4, 5).reshape(64, 16, ch)
    shard = shard.reshape(-1, 1, 8, half)
    quarters = [shard] + [moved(shard, lambda y, z, x, c, k=k: (y, z ^ k, x, c)) for k in (2, 4, 6)]
    for bit in (0, 1):
        turned = (lax.axis_index("z") >> (bit + 1)) & 1 == 1
        quarters = [jnp.where(turned, quarters[q ^ (1 << bit)], quarters[q]) for q in range(4)]
    shard = jnp.concatenate(quarters, axis=1)
    shard = joined(shard, from_z(shard), lax.axis_index("z") & 1)
    shard = shard.reshape(-1, 8, 8, half)
    shard, cells = lax.optimization_barrier((shard, cells))
    cells = lax.all_to_all(cells, PEERS, 0, 0).reshape(ROWS, LINE, ch)

    near_half = jnp.stack([shard[:TAPS], from_y(shard[:TAPS])])
    rest = shard[TAPS:]
    first = jnp.stack([rest, from_x(rest, 0)])
    second = from_x(first, 1)
    first_y = from_y(first)
    t_first = jnp.stack([near_half, from_x(near_half, 0)])
    t_second = from_x(t_first, 1)
    tight_parts = [t_first, t_second, from_core(t_first), from_core(t_second)]
    second, first_y = lax.optimization_barrier((second, first_y))
    own = [first, second, first_y, from_y(second)]
    late, cells = lax.optimization_barrier((own[3], cells))
    parts = own + [from_core(late if n == 3 else piece) for n, piece in enumerate(own)]

    near = block(near_kernel, cells, tight_parts, 1, where, False)
    out = block(far_kernel, near, parts, 4, where, True)
    out = lax.all_to_all(out.reshape(64, 16, ch), PEERS, 0, 0)
    return out.reshape(s, i, 8, 8, PAIR, ch).transpose(0, 1, 3, 2, 4, 5).reshape(inputs.shape)


def solution(mesh):
    grid = Mesh(mesh.devices.reshape(SIZES), AXES)
    rows, columns = ("ylo", "z", "x"), ("yhi", "core")
    placed = (
        P(None, rows, columns, None),
        P(None, None, rows, None),
        P(None, None, rows, None),
        P(None, rows),
        P(rows, None),
    )
    return jax.shard_map(shards, mesh=grid, in_specs=placed, out_specs=P(None, rows, columns, None), check_vma=False)
```
